32 devices in a mesh: scene: 4 (over y, x), region: 8 (over z, core).
Axes of the slice: x: 2, y: 2, z: 4, core: 2. Of those that a mesh axis runs over, the one named last changes fastest.
Arguments:
- features: bfloat16 [4, 8, 1728, 128], P('scene', 'region'), may hold values from -6 to 6
- voxel_mask: int32 [4, 8, 1728], P('scene', 'region'), may hold values 0 or 1
- cotangent: bfloat16 [4, 8, 1728, 128], P('scene', 'region'), may hold values from -6 to 6
- norm_gain: float32 [128], replicated, may hold values from 0.1 to 1.9
- conv_weight: bfloat16 [27, 128, 128], replicated, may hold values from -0.109375 to 0.109375
- block_owner: int32 [4, 8], P('scene'), may hold values from 0 to 7, each once within a row
Outputs:
- block_output: bfloat16 [4, 8, 1728, 128], P('scene', 'region')
- input_grad: bfloat16 [4, 8, 1728, 128], P('scene', 'region')
- weight_update: float32 [3456, 128], P('region')
The draws below stay inside these ranges and needn't reach their ends.
Inputs may be any that keep to these rules, and one draw needn't show every extreme that they name: `block_owner`: each row names every slot of the scene exactly once.
All inputs are finite; a program needn't handle non-finite values. No bound on the sum of `voxel_mask` on one device may be relied on, other than what follows from the above.
Results may differ from the reference program's by a relative error of at most 0.0029.
Values may be sent and summed in bfloat16 or wider, within the bound.
A program may use at most 128 MiB of HBM per device.

```python
import math
import jax
import jax.numpy as jnp
from jax import lax

C = 128
BS = 12
TAPS = 27
GY = 4
GZ = 2
GX = 1
SLOTS = 8
SCENES = 4
VOX = 1728


def place_ends(result, stream_key, low, high):
    longest = result.shape.index(max(result.shape))
    spots = []
    for shift in (0, 1):
        where = [jax.random.randint(jax.random.fold_in(stream_key, axis), (), 0, length) for axis, length in enumerate(result.shape)]
        where[longest] = (where[longest] + shift) % result.shape[longest]
        spots.append(tuple(where))
    return result.at[spots[0]].set(low).at[spots[1]].set(high)


def block_scale(stream_key, dims, shards, smallest, high):
    gain = 1.0
    for dim, blocks in shards:
        steps = jax.random.uniform(jax.random.fold_in(jax.random.fold_in(stream_key, 6), dim), (blocks,), jnp.float32, smallest / len(shards), high / len(shards))
        gain = gain * jnp.repeat(jnp.exp(steps), dims[dim] // blocks).reshape((-1,) + (1,) * (len(dims) - 1 - dim))
    return gain


def centred(own_key, extent, scale, most, pieces=(), kind=jnp.bfloat16):
    entries = scale * jax.random.normal(own_key, extent, jnp.float32)
    if pieces:
        entries = entries * block_scale(own_key, extent, pieces, -0.22, 0.18)
    return jnp.clip(entries, -most, most).astype(kind)


def setup_inputs(seed: int = 0) -> dict:
    key_list = jax.random.split(jax.random.key(seed), 7)
    return {
        "features": centred(key_list[0], (SCENES, SLOTS, VOX, C), 1.0, 6.0, ((0, 4), (1, 8))),
        "voxel_mask": place_ends((jax.random.randint(key_list[1], (SCENES, SLOTS, VOX), 0, 2) < 1).astype(jnp.int32), jax.random.fold_in(key_list[1], 1), 0, 1),
        "cotangent": centred(key_list[2], (SCENES, SLOTS, VOX, C), 1.0, 6.0, ((0, 4), (1, 8))),
        "norm_gain": jnp.clip(1.0 + 0.18 * jax.random.normal(key_list[3], (C,), jnp.float32), 0.1, 1.9),
        "conv_weight": centred(key_list[4], (TAPS, C, C), (TAPS * C) ** -0.5, 0.109375),
        "block_owner": jax.vmap(lambda own: jax.random.permutation(own, SLOTS))(jax.random.split(key_list[5], SCENES)).reshape((SCENES, SLOTS)).astype(jnp.int32),
    }


NORM_EPSILON = 1e-06
OFFSETS = [(a, b, c) for a in (-1, 0, 1) for b in (-1, 0, 1) for c in (-1, 0, 1)]

def to_grid(blocks):
    width = blocks.shape[-1]
    cube = blocks.reshape(GX, GY, GZ, BS, BS, BS, width)
    cube = cube.transpose(0, 3, 1, 4, 2, 5, 6).reshape(GX * BS, GY * BS, GZ * BS, width)
    return jnp.pad(cube, ((1, 1), (1, 1), (1, 1), (0, 0)))

def scene_pass(x_blocks, mask_blocks, cot_blocks, norm_gain, conv_weight):
    inputs = x_blocks.astype(jnp.float32)
    mask_col = mask_blocks.astype(jnp.float32)[..., None]
    rinv = lax.rsqrt(lax.optimization_barrier(jnp.mean(inputs * inputs, axis=-1, keepdims=True)) + NORM_EPSILON)
    normed = inputs * rinv
    pre = normed * norm_gain
    activity = (jax.nn.silu(pre) * mask_col).astype(jnp.bfloat16)
    grad_out = cot_blocks * mask_blocks.astype(jnp.bfloat16)[..., None]
    act_grid = to_grid(activity)
    grad_grid = to_grid(grad_out)
    width = x_blocks.shape[-1]

    def step(weight_grad, block_index):
        block_x = block_index // (GY * GZ)
        block_y = block_index // GZ % GY
        block_z = block_index % GZ
        zero_index = jnp.zeros((), jnp.int32)
        starts = (block_x * BS, block_y * BS, block_z * BS, zero_index)
        window_act = lax.dynamic_slice(act_grid, starts, (BS + 2, BS + 2, BS + 2, width))
        window_grad = lax.dynamic_slice(grad_grid, starts, (BS + 2, BS + 2, BS + 2, width))
        grad_block = lax.dynamic_index_in_dim(grad_out, block_index, 0, keepdims=False)
        forward = jnp.zeros((BS * BS * BS, width), jnp.float32)
        backward = jnp.zeros((BS * BS * BS, width), jnp.float32)
        terms = []
        for tap_index, (shift_x, shift_y, shift_z) in enumerate(OFFSETS):
            window = window_act[1 + shift_x:1 + shift_x + BS, 1 + shift_y:1 + shift_y + BS, 1 + shift_z:1 + shift_z + BS].reshape(-1, width)
            forward = forward + jnp.dot(window, conv_weight[tap_index], preferred_element_type=jnp.float32)
            mirror = window_grad[1 - shift_x:1 - shift_x + BS, 1 - shift_y:1 - shift_y + BS, 1 - shift_z:1 - shift_z + BS].reshape(-1, width)
            backward = backward + lax.dot_general(mirror, conv_weight[tap_index], (((1,), (1,)), ((), ())), preferred_element_type=jnp.float32)
            terms.append(lax.dot_general(window, grad_block, (((0,), (0,)), ((), ())), preferred_element_type=jnp.float32))
        return (weight_grad + jnp.stack(terms), (forward, backward))
    start_grad = jnp.zeros((TAPS, width, width), jnp.float32)
    weight_grad, (forward, backward) = lax.scan(step, start_grad, jnp.arange(SLOTS, dtype=jnp.int32))
    block_output = (inputs + forward * mask_col).astype(jnp.bfloat16)
    slope = jax.nn.sigmoid(pre)
    dnorm = backward * mask_col * (slope * (1.0 + pre * (1.0 - slope))) * norm_gain
    dinput = rinv * (dnorm - normed * lax.optimization_barrier(jnp.mean(dnorm * normed, axis=-1, keepdims=True)))
    input_grad = (cot_blocks.astype(jnp.float32) + dinput).astype(jnp.bfloat16)
    return (block_output, input_grad, weight_grad)

def reference(features, voxel_mask, cotangent, norm_gain, conv_weight, block_owner):
    limit = math.sqrt(TAPS * C * C)
    outputs = []
    gradients = []
    update = jnp.zeros((TAPS, C, C), jnp.float32)
    for scene_index in range(SCENES):
        owner_row = block_owner[scene_index]
        block_output, input_grad, weight_grad = scene_pass(features[scene_index][owner_row], voxel_mask[scene_index][owner_row], cotangent[scene_index][owner_row], norm_gain, conv_weight)
        outputs.append(jnp.zeros_like(features[scene_index]).at[owner_row].set(block_output))
        gradients.append(jnp.zeros_like(cotangent[scene_index]).at[owner_row].set(input_grad))
        factor = jnp.minimum(1.0, limit / jnp.sqrt(jnp.sum(weight_grad * weight_grad)))
        update = update + factor * weight_grad
    return (jnp.stack(outputs), jnp.stack(gradients), (update / SCENES).reshape(TAPS * C, C))
```

```python
import functools
import math

import jax
import jax.numpy as jnp
import numpy as np
from jax import lax
from jax.experimental import pallas as pl
from jax.experimental.pallas import tpu as pltpu
from jax.sharding import PartitionSpec as P

BS = 12
TAPS = 27
GY = 4
GZ = 2


NORM_EPSILON = 1e-06
OFFSETS = [(a, b, c) for a in (-1, 0, 1) for b in (-1, 0, 1) for c in (-1, 0, 1)]
DIRECTIONS = [
    item
    for level in (1, 2, 3)
    for item in OFFSETS
    if abs(item[0]) + abs(item[1]) + abs(item[2]) == level
]
COLUMNS = [(a, b) for a in (-1, 0, 1) for b in (-1, 0, 1)]


def side_range(component, edge):
    if component == 1:
        return (edge - 1, edge)
    if component == -1:
        return (0, 1)
    return (0, edge)


def halo_range(component, edge):
    if component == 1:
        return (edge + 1, edge + 2)
    if component == -1:
        return (0, 1)
    return (1, edge + 1)


def slab_count(direction, edge):
    total = 1
    for component in direction:
        total = total * (1 if component != 0 else edge)
    return total


def row_directions(edge, region_count):
    labels = []
    for position, direction in enumerate(DIRECTIONS):
        labels = labels + [position] * slab_count(direction, edge)
    per_peer = -(-len(labels) // region_count)
    labels = labels + [len(DIRECTIONS)] * (per_peer * region_count - len(labels))
    return (np.array(labels, dtype=np.int32).reshape(per_peer, region_count), len(labels), per_peer)


def holder_table(owner_row, region_count):
    slot_ids = jnp.arange(region_count, dtype=jnp.int32)
    block_of = jnp.sum(
        jnp.where(owner_row[None, :] == slot_ids[:, None], slot_ids[None, :], 0), axis=1
    )
    layer = GY * GZ
    across = region_count // layer
    block_x = block_of // layer
    block_y = block_of // GZ % GY
    block_z = block_of % GZ
    columns = []
    for direction in DIRECTIONS:
        near_x = block_x + direction[0]
        near_y = block_y + direction[1]
        near_z = block_z + direction[2]
        inside = (
            (near_x >= 0)
            & (near_x < across)
            & (near_y >= 0)
            & (near_y < GY)
            & (near_z >= 0)
            & (near_z < GZ)
        )
        target = jnp.clip(near_x * layer + near_y * GZ + near_z, 0, region_count - 1)
        holder = jnp.take(owner_row, target, axis=0)
        columns.append(jnp.where(inside, holder, -1))
    columns.append(jnp.full((region_count,), -1, jnp.int32))
    return jnp.stack(columns, axis=1)


def route_plan(owner_row, region_count):
    labels, padded_rows, per_peer = row_directions(BS, region_count)
    myself = lax.axis_index("region")
    labels_now = lax.dynamic_index_in_dim(jnp.asarray(labels), myself, 1, keepdims=False)
    holders = holder_table(owner_row, region_count)
    sources = jnp.take(holders, labels_now, axis=1)
    valid = sources >= 0
    positions = jnp.arange(per_peer, dtype=jnp.int32)[None, :]
    source_rows = jnp.where(valid, sources * per_peer + positions, 0).reshape(-1)
    return (source_rows, valid.astype(jnp.bfloat16), per_peer)


def dealt_shell(cube, region_count, per_peer):
    edge = cube.shape[0]
    width = cube.shape[3]
    pieces = []
    for direction in DIRECTIONS:
        spans = [side_range(-component, edge) for component in direction]
        pieces.append(
            cube[
                spans[0][0] : spans[0][1], spans[1][0] : spans[1][1], spans[2][0] : spans[2][1]
            ].reshape(-1, width)
        )
    rows = jnp.concatenate(pieces, axis=0)
    rows = jnp.pad(rows, ((0, per_peer * region_count - rows.shape[0]), (0, 0)))
    return rows.reshape(per_peer, region_count, width).transpose(1, 0, 2)


def pick_rows(holdings, plan):
    source_rows, valid, per_peer = plan
    width = holdings.shape[2]
    flat = holdings.reshape(-1, width)
    picked = jnp.take(flat, source_rows, axis=0).reshape(holdings.shape[0], per_peer, width)
    return picked * valid[..., None]


def relay(plan, cube, region_count):
    dealt = lax.all_to_all(
        dealt_shell(cube, region_count, plan[2]), "region", split_axis=0, concat_axis=0, tiled=True
    )
    return lax.all_to_all(pick_rows(dealt, plan), "region", split_axis=0, concat_axis=0, tiled=True)


def assemble(received, cube):
    edge = cube.shape[0]
    width = cube.shape[3]
    whole = received.transpose(1, 0, 2).reshape(-1, width)
    padded = jnp.pad(cube, ((1, 1), (1, 1), (1, 1), (0, 0)))
    offset = 0
    for direction in DIRECTIONS:
        spans = [halo_range(component, edge) for component in direction]
        lengths = [upper - lower for lower, upper in spans]
        count = lengths[0] * lengths[1] * lengths[2]
        piece = whole[offset : offset + count].reshape(lengths[0], lengths[1], lengths[2], width)
        padded = padded.at[
            spans[0][0] : spans[0][1], spans[1][0] : spans[1][1], spans[2][0] : spans[2][1]
        ].set(piece)
        offset = offset + count
    return padded


def column_window(padded, shift_x, shift_y, edge, width):
    column = padded[1 + shift_x : 1 + shift_x + edge, 1 + shift_y : 1 + shift_y + edge]
    return jnp.concatenate(
        [column[:, :, 1 + shift_z : 1 + shift_z + edge] for shift_z in (-1, 0, 1)], axis=-1
    ).reshape(-1, 3 * width)


def convolve(padded_act, padded_grad, grad_block, conv_weight):
    edge = padded_act.shape[0] - 2
    width = padded_act.shape[3]
    forward = jnp.zeros((edge * edge * edge, width), jnp.float32)
    backward = jnp.zeros((edge * edge * edge, width), jnp.float32)
    terms = []
    for group_index, (shift_x, shift_y) in enumerate(COLUMNS):
        group_weight = conv_weight[3 * group_index : 3 * group_index + 3]
        window = column_window(padded_act, shift_x, shift_y, edge, width)
        forward = forward + jnp.dot(
            window, group_weight.reshape(3 * width, width), preferred_element_type=jnp.float32
        )
        mirror_column = padded_grad[
            1 - shift_x : 1 - shift_x + edge, 1 - shift_y : 1 - shift_y + edge
        ]
        mirror = jnp.concatenate(
            [mirror_column[:, :, 1 - shift_z : 1 - shift_z + edge] for shift_z in (-1, 0, 1)],
            axis=-1,
        ).reshape(-1, 3 * width)
        backward = backward + jnp.dot(
            mirror,
            group_weight.transpose(0, 2, 1).reshape(3 * width, width),
            preferred_element_type=jnp.float32,
        )
        terms.append(
            lax.dot_general(
                window, grad_block, (((0,), (0,)), ((), ())), preferred_element_type=jnp.float32
            )
        )
    return (forward, backward, jnp.concatenate(terms, axis=0).reshape(TAPS, width, width))


def body(features, voxel_mask, cotangent, norm_gain, conv_weight, block_owner):
    width = features.shape[-1]
    region_count = lax.axis_size("region")
    plan = route_plan(block_owner[0], region_count)
    inputs = features[0, 0].astype(jnp.float32)
    mask_col = voxel_mask[0, 0].astype(jnp.float32)[:, None]
    rinv = lax.rsqrt(jnp.mean(inputs * inputs, axis=-1, keepdims=True) + NORM_EPSILON)
    normed = inputs * rinv
    pre = normed * norm_gain
    activity = (jax.nn.silu(pre) * mask_col).astype(jnp.bfloat16)
    grad_out = cotangent[0, 0] * voxel_mask[0, 0].astype(jnp.bfloat16)[:, None]
    act_cube = activity.reshape(BS, BS, BS, width)
    grad_cube = grad_out.reshape(BS, BS, BS, width)
    act_recv = relay(plan, act_cube, region_count)
    grad_recv = relay(plan, grad_cube, region_count)
    padded_act = assemble(act_recv, act_cube)
    padded_grad = assemble(grad_recv, grad_cube)
    forward, backward, weight_grad = convolve(padded_act, padded_grad, grad_out, conv_weight)
    block_output = (inputs + forward * mask_col).astype(jnp.bfloat16)
    slope = jax.nn.sigmoid(pre)
    dnorm = backward * mask_col * (slope * (1.0 + pre * (1.0 - slope))) * norm_gain
    dinput = rinv * (dnorm - normed * jnp.mean(dnorm * normed, axis=-1, keepdims=True))
    input_grad = (cotangent[0, 0].astype(jnp.float32) + dinput).astype(jnp.bfloat16)
    flat_grad = weight_grad.reshape(-1, width)
    share_rows = flat_grad.shape[0] // region_count
    limit = math.sqrt(flat_grad.shape[0] * width)
    summed = lax.psum(flat_grad, "region")
    total_squares = jnp.sum(summed * summed)
    share = lax.dynamic_slice_in_dim(summed, lax.axis_index("region") * share_rows, share_rows, 0)
    factor = jnp.minimum(1.0, limit / jnp.sqrt(total_squares))
    update = lax.psum(share * factor, "scene") / lax.axis_size("scene")
    return (block_output.reshape(features.shape), input_grad.reshape(cotangent.shape), update)


PLANE = BS * BS
ZPAD = 16
ROWS = BS * ZPAD
WIDE = (BS + 2) * ZPAD
EDGE_ROWS = 4 * BS
STACK = 256
FACE_A, FACE_D, FACE_C, FACE_B = 0, BS, 2 * BS, 3 * BS


def extract_table():
    table = np.zeros((EDGE_ROWS, PLANE), np.float32)
    for i in range(BS):
        table[FACE_A + i, i] = 1
        table[FACE_D + i, i * BS + BS - 1] = 1
        table[FACE_C + i, i * BS] = 1
        table[FACE_B + i, (BS - 1) * BS + i] = 1
    return table


def spread_table():
    ym, yp, zn = PLANE, PLANE + 16, PLANE + 32
    ymz, ypz = zn + EDGE_ROWS, zn + EDGE_ROWS + 16
    table = np.zeros((GZ, 3, BS + 2, ZPAD, STACK), np.float32)
    for bz in range(GZ):
        for c in range(3):
            for y in range(-1, BS + 1):
                for row in range(BS + 2):
                    z = row - 1 + c - 1
                    if z < -1 or z > BS:
                        continue
                    y_in, z_in = 0 <= y < BS, 0 <= z < BS
                    if not z_in and (z < 0) != (bz == 1):
                        continue
                    near = 0 if z > 0 else BS - 1
                    if y_in and z_in:
                        col = y * BS + z
                    elif z_in:
                        col = ym + FACE_B - 32 + z if y < 0 else yp + FACE_A + z
                    elif y_in:
                        col = zn + (FACE_C if z > 0 else FACE_D) + y
                    else:
                        col = ymz + FACE_B - 32 + near if y < 0 else ypz + FACE_A + near
                    table[bz, c, y + 1, row, col] = 1
    return table


def fused_kernel(
    feat, mask, cot, gain, weight, near, extract, spread, own_spread, squeeze,
    out, grad_in, update,
    g_msg, a_msg, g_stack, a_stack, g_wide, a_wide, own_wide, own_turned,
    normed_s, slope_s, rinv_s, part, from_twin, pair16, pair_own, from_z, squares, shares, factors,
    halo_send, halo_recv, twin_send, twin_recv, z_send, z_recv, sq_send, sq_recv, sh_send, sh_recv, fa_send, fa_recv,
):
    f32, bf16 = jnp.float32, jnp.bfloat16
    me = lax.axis_index("region")
    scene = lax.axis_index("scene")
    core = lax.rem(me, 2)
    chip = lax.div(me, 2)
    chips = GY * GZ // 2
    twin = 2 * chip + 1 - core
    share_rows = TAPS * 128 // (GY * GZ)

    def remote(src, dst, send, recv, **where):
        return pltpu.make_async_remote_copy(
            src_ref=src, dst_ref=dst, send_sem=send, recv_sem=recv,
            device_id=where, device_id_type=pl.DeviceIdType.MESH,
        )

    barrier = pltpu.get_barrier_semaphore()
    for k in range(1, 8):
        pl.semaphore_signal(barrier, inc=1, device_id={"region": lax.rem(me + k, 8)}, device_id_type=pl.DeviceIdType.MESH)
    for k in range(1, 4):
        pl.semaphore_signal(barrier, inc=1, device_id={"scene": lax.rem(scene + k, 4)}, device_id_type=pl.DeviceIdType.MESH)

    def at_plane(x, step):
        return pl.ds(pl.multiple_of(x * step, step), step)

    def grad_plane(x, carry):
        rows = at_plane(x, PLANE)
        g = cot[rows, :] * mask[rows, :]
        g_stack[x, 0:PLANE, :] = g
        g_msg[me, at_plane(x, EDGE_ROWS), :] = jnp.dot(extract[...], g, preferred_element_type=f32).astype(bf16)
        return carry

    lax.fori_loop(0, BS, grad_plane, 0, unroll=2)
    pl.semaphore_wait(barrier, 10)

    def halo_copy(which, msg, index, slot, target):
        return remote(msg.at[slot], msg.at[slot], halo_send.at[which, index], halo_recv.at[which, slot], region=target)

    def start_halo(which, msg):
        for k in (2, 1, 3):
            halo_copy(which, msg, k - 1, me, 2 * lax.rem(chip + k, chips) + core).start()
        halo_copy(which, msg, 3, me, twin).start()

    def pass_halo(which, msg):
        for k in (1, 3, 2):
            slot = 2 * lax.rem(chip + chips - k, chips) + core
            halo_copy(which, msg, 0, slot, twin).wait_recv()
            halo_copy(which, msg, 3 + k, slot, twin).start()

    def end_halo(which, msg):
        for k in range(4):
            slot = 2 * lax.rem(chip + k, chips) + 1 - core
            halo_copy(which, msg, 0, slot, twin).wait_recv()

    start_halo(0, g_msg)
    g_msg[8] = jnp.zeros(g_msg.shape[1:], bf16)
    a_msg[8] = jnp.zeros(a_msg.shape[1:], bf16)

    def act_plane(x, carry):
        rows = at_plane(x, PLANE)
        inputs = feat[rows, :].astype(f32)
        rinv = lax.rsqrt(jnp.mean(inputs * inputs, axis=-1, keepdims=True) + NORM_EPSILON)
        normed = inputs * rinv
        pre = normed * gain[...]
        slope = 1.0 / (1.0 + jnp.exp(-pre))
        kept = mask[rows, :].astype(f32)
        act = (pre * slope * kept).astype(bf16)
        normed_s[rows, :] = normed
        slope_s[rows, :] = kept * (slope * (1.0 + pre * (1.0 - slope))) * gain[...]
        rinv_s[rows, :] = jnp.broadcast_to(rinv, normed.shape)
        a_stack[x, 0:PLANE, :] = act
        a_msg[me, at_plane(x, EDGE_ROWS), :] = jnp.dot(extract[...], act, preferred_element_type=f32).astype(bf16)
        return carry

    lax.fori_loop(0, BS, act_plane, 0, unroll=2)
    start_halo(1, a_msg)

    def own_plane(x, carry):
        moved = jnp.dot(own_spread[...], a_stack[x, 0:PLANE, :], preferred_element_type=f32).astype(bf16)
        for c in range(3):
            own_wide[at_plane(x, ROWS), c * 128 : (c + 1) * 128] = moved[c * ROWS : (c + 1) * ROWS]
        return carry

    lax.fori_loop(0, BS, own_plane, 0, unroll=2)
    turn = 4 * ROWS
    for i in range(3):
        for c in range(3):
            own_turned[c * 128 : (c + 1) * 128, i * turn : (i + 1) * turn] = own_wide[
                i * turn : (i + 1) * turn, c * 128 : (c + 1) * 128
            ].T

    def widen(msg, stack, wide):
        wide[0] = jnp.zeros(wide.shape[1:], bf16)
        wide[BS + 1] = jnp.zeros(wide.shape[1:], bf16)

        def plane(x, carry):
            low = pl.ds(pl.multiple_of(x * EDGE_ROWS, 16), 16)
            high = pl.ds(pl.multiple_of(x * EDGE_ROWS + 32, 16), 16)
            stack[x, PLANE : PLANE + 16, :] = msg[near[0], high, :]
            stack[x, PLANE + 16 : PLANE + 32, :] = msg[near[1], low, :]
            stack[x, PLANE + 32 : PLANE + 80, :] = msg[near[2], at_plane(x, EDGE_ROWS), :]
            stack[x, PLANE + 80 : PLANE + 96, :] = msg[near[3], high, :]
            stack[x, PLANE + 96 : PLANE + 112, :] = msg[near[4], low, :]
            moved = jnp.dot(spread[near[5]], stack[x], preferred_element_type=f32).astype(bf16)
            for c in range(3):
                wide[x + 1, :, c * 128 : (c + 1) * 128] = moved[c * WIDE : (c + 1) * WIDE]
            return carry

        lax.fori_loop(0, BS, plane, 0, unroll=2)

    pass_halo(0, g_msg)
    end_halo(0, g_msg)
    widen(g_msg, g_stack, g_wide)

    def window(a, b):
        return g_wide[1 - a : 1 - a + BS, (1 - b) * ZPAD : (1 - b) * ZPAD + ROWS, 128:256].reshape(BS * ROWS, 128)

    for first in range(0, 9, 2):
        group = list(range(first, min(first + 2, 9)))
        side = [window(*COLUMNS[i]) for i in group]
        rhs = jnp.concatenate(side, axis=1) if len(side) > 1 else side[0]
        term = jnp.dot(own_turned[...], rhs, preferred_element_type=f32)
        for j, i in enumerate(group):
            part[3 * i * 128 : (3 * i + 3) * 128, :] = term[:, j * 128 : (j + 1) * 128]

    def share_of(index):
        return pl.ds(pl.multiple_of(index * share_rows, 16), share_rows)

    def twin_copy(q):
        return remote(part.at[share_of(2 * q + 1 - core)], from_twin.at[q], twin_send.at[q], twin_recv.at[q], region=twin)

    for q in range(chips):
        twin_copy(q).start()
    pass_halo(1, a_msg)

    def z_copy(k):
        target = lax.rem(chip + k, chips)
        return remote(pair16.at[target], from_z.at[k - 1], z_send.at[k - 1], z_recv.at[k - 1], region=2 * target + core)

    for q in range(chips):
        twin_copy(q).wait_recv()
    for k in (2, 1, 3):
        q = lax.rem(chip + k, chips)
        pair16[q] = (part[share_of(2 * q + core), :] + from_twin[q]).astype(bf16)
        z_copy(k).start()
    pair_own[...] = part[share_of(me), :] + from_twin[chip]

    count = 3

    def convolve_planes(wide, taps, x0, transposed):
        total = None
        for a in range(3):
            lhs = jnp.concatenate(
                [wide[pl.ds(x0 + a, count), b * ZPAD : b * ZPAD + ROWS, :].reshape(count * ROWS, 384) for b in range(3)],
                axis=1,
            )
            if transposed:
                rhs = jnp.concatenate([taps[26 - 9 * a - j] for j in range(9)], axis=1)
                term = lax.dot_general(lhs, rhs, (((1,), (1,)), ((), ())), preferred_element_type=f32)
            else:
                term = jnp.dot(lhs, taps[9 * a : 9 * a + 9].reshape(9 * 128, 128), preferred_element_type=f32)
            total = term if total is None else total + term
        planes = []
        for i in range(count):
            piece = total[i * ROWS : (i + 1) * ROWS]
            high = piece.astype(bf16)
            rest = (piece - high.astype(f32)).astype(bf16)
            planes.append(jnp.dot(squeeze[...], jnp.concatenate([high, rest], axis=0), preferred_element_type=f32))
        return planes

    def backward_planes(step, carry):
        x0 = step * count
        for i, back in enumerate(convolve_planes(g_wide, weight, x0, True)):
            rows = at_plane(x0 + i, PLANE)
            normed = normed_s[rows, :]
            dnorm = back * slope_s[rows, :]
            level = jnp.mean(dnorm * normed, axis=-1, keepdims=True)
            grad_in[rows, :] = (cot[rows, :].astype(f32) + rinv_s[rows, :] * (dnorm - normed * level)).astype(bf16)
        return carry

    lax.fori_loop(0, BS // count, backward_planes, 0)

    end_halo(1, a_msg)
    widen(a_msg, a_stack, a_wide)

    def z_wait(k):
        z_copy(k).wait_recv()

    for k in (1, 3, 2):
        z_wait(k)
    share = pair_own[...] + from_z[0].astype(f32) + from_z[1].astype(f32) + from_z[2].astype(f32)
    squares[me] = jnp.sum((share * share).reshape(share_rows // 8, 8, 128), axis=0)
    shares[scene] = share.astype(bf16)

    def sq_copy(k):
        return remote(squares.at[me], squares.at[me], sq_send.at[k - 1], sq_recv.at[k - 1], region=lax.rem(me + k, 8))

    def sq_arrival(k):
        slot = lax.rem(me + 8 - k, 8)
        return remote(squares.at[slot], squares.at[slot], sq_send.at[k - 1], sq_recv.at[k - 1], region=slot)

    def scene_copy(buf, send, recv, k):
        return remote(buf.at[scene], buf.at[scene], send.at[k - 1], recv.at[k - 1], scene=lax.rem(scene + k, 4))

    def scene_arrival(buf, send, recv, k):
        slot = lax.rem(scene + 4 - k, 4)
        return remote(buf.at[slot], buf.at[slot], send.at[k - 1], recv.at[k - 1], scene=slot)

    for k in range(1, 8):
        sq_copy(k).start()
    for k in range(1, 4):
        scene_copy(shares, sh_send, sh_recv, k).start()

    def forward_planes(step, carry):
        x0 = step * count
        for i, ahead in enumerate(convolve_planes(a_wide, weight, x0, False)):
            rows = at_plane(x0 + i, PLANE)
            out[rows, :] = (feat[rows, :].astype(f32) + ahead * mask[rows, :].astype(f32)).astype(bf16)
        return carry

    lax.fori_loop(0, 1, forward_planes, 0)
    for k in range(1, 8):
        sq_arrival(k).wait_recv()
    total = jnp.sum(jnp.sum(squares[...], axis=0), keepdims=True)
    limit = math.sqrt(TAPS * 128 * 128)
    factors[scene] = jnp.broadcast_to(jnp.minimum(1.0, limit * lax.rsqrt(total)), (8, 128))
    for k in range(1, 4):
        scene_copy(factors, fa_send, fa_recv, k).start()
    lax.fori_loop(1, BS // count, forward_planes, 0)
    for k in range(1, 4):
        scene_arrival(shares, sh_send, sh_recv, k).wait_recv()
        scene_arrival(factors, fa_send, fa_recv, k).wait_recv()
    result = jnp.zeros((share_rows, 128), f32)
    for s in range(4):
        result = result + factors[s, 0:1, :] * shares[s].astype(f32)
    update[...] = result * 0.25

    for which, msg in ((0, g_msg), (1, a_msg)):
        for index in range(7):
            halo_copy(which, msg, index, me, twin).wait_send()
    for q in range(chips):
        twin_copy(q).wait_send()
    for k in range(1, 4):
        z_copy(k).wait_send()
        scene_copy(shares, sh_send, sh_recv, k).wait_send()
        scene_copy(factors, fa_send, fa_recv, k).wait_send()
    for k in range(1, 8):
        sq_copy(k).wait_send()


def fused_body(features, voxel_mask, cotangent, norm_gain, conv_weight, block_owner):
    f32, bf16 = jnp.float32, jnp.bfloat16
    width = features.shape[-1]
    slots = lax.axis_size("region")
    spread = spread_table()
    own = spread[0, :, 1 : 1 + BS, :, :PLANE].reshape(3 * ROWS, PLANE)
    squeeze = np.zeros((BS, BS, BS, ZPAD), np.float32)
    for y in range(BS):
        for z in range(BS):
            squeeze[y, z, y, z + 1] = 1
    squeeze = squeeze.reshape(PLANE, ROWS)
    squeeze = np.concatenate([squeeze, squeeze], axis=1)
    spread = spread.reshape(GZ, 3 * WIDE, STACK)
    owner = block_owner[0]
    block = jnp.sum(jnp.where(owner == lax.axis_index("region"), jnp.arange(slots, dtype=jnp.int32), 0))
    by, bz = block // GZ, block % GZ

    def holder(y, z):
        inside = (y >= 0) & (y < GY)
        return jnp.where(inside, owner[jnp.clip(y * GZ + z, 0, slots - 1)], slots)

    near = jnp.stack(
        [holder(by - 1, bz), holder(by + 1, bz), holder(by, 1 - bz), holder(by - 1, 1 - bz), holder(by + 1, 1 - bz), bz]
    ).astype(jnp.int32)
    voxels = BS * BS * BS
    mask = jnp.broadcast_to(voxel_mask[0, 0].astype(bf16)[:, None], (voxels, width))
    vmem = pl.BlockSpec(memory_space=pltpu.VMEM)
    share_rows = TAPS * width // slots
    sem = pltpu.SemaphoreType.DMA
    out, grad_in, update = pl.pallas_call(
        fused_kernel,
        out_shape=(
            jax.ShapeDtypeStruct((voxels, width), bf16),
            jax.ShapeDtypeStruct((voxels, width), bf16),
            jax.ShapeDtypeStruct((share_rows, width), f32),
        ),
        in_specs=[vmem] * 5 + [pl.BlockSpec(memory_space=pltpu.SMEM)] + [vmem] * 4,
        out_specs=(vmem, vmem, vmem),
        scratch_shapes=[
            pltpu.VMEM((slots + 1, BS * EDGE_ROWS, width), bf16),
            pltpu.VMEM((slots + 1, BS * EDGE_ROWS, width), bf16),
            pltpu.VMEM((BS, STACK, width), bf16),
            pltpu.VMEM((BS, STACK, width), bf16),
            pltpu.VMEM((BS + 2, WIDE, 3 * width), bf16),
            pltpu.VMEM((BS + 2, WIDE, 3 * width), bf16),
            pltpu.VMEM((BS * ROWS, 3 * width), bf16),
            pltpu.VMEM((3 * width, BS * ROWS), bf16),
            pltpu.VMEM((voxels, width), f32),
            pltpu.VMEM((voxels, width), f32),
            pltpu.VMEM((voxels, width), f32),
            pltpu.VMEM((TAPS * width, width), f32),
            pltpu.VMEM((slots // 2, share_rows, width), f32),
            pltpu.VMEM((slots // 2, share_rows, width), bf16),
            pltpu.VMEM((share_rows, width), f32),
            pltpu.VMEM((slots // 2 - 1, share_rows, width), bf16),
            pltpu.VMEM((slots, 8, width), f32),
            pltpu.VMEM((4, share_rows, width), bf16),
            pltpu.VMEM((4, 8, width), f32),
            sem((2, 7)), sem((2, slots)),
            sem((slots // 2,)), sem((slots // 2,)),
            sem((3,)), sem((3,)),
            sem((7,)), sem((7,)),
            sem((3,)), sem((3,)),
            sem((3,)), sem((3,)),
        ],
        compiler_params=pltpu.CompilerParams(
            collective_id=0, has_side_effects=True, vmem_limit_bytes=50 * 1024 * 1024
        ),
        cost_estimate=pl.CostEstimate(flops=5_000_000_000, bytes_accessed=4_000_000, transcendentals=300_000),
    )(
        features[0, 0], mask, cotangent[0, 0], norm_gain[None, :], conv_weight, near,
        jnp.asarray(extract_table(), bf16), jnp.asarray(spread, bf16), jnp.asarray(own, bf16), jnp.asarray(squeeze, bf16),
    )
    return (out.reshape(features.shape), grad_in.reshape(cotangent.shape), update)


def solution(mesh):
    in_specs = (
        P("scene", "region", None, None),
        P("scene", "region", None),
        P("scene", "region", None, None),
        P(),
        P(),
        P("scene", None),
    )
    out_specs = (
        P("scene", "region", None, None),
        P("scene", "region", None, None),
        P("region", None),
    )
    chosen = fused_body if mesh.shape["region"] == GY * GZ else body
    return jax.shard_map(chosen, mesh=mesh, in_specs=in_specs, out_specs=out_specs, check_vma=False)
```

```python
import functools
import math

import jax
import jax.numpy as jnp
import numpy as np
from jax import lax
from jax.experimental import pallas as pl
from jax.experimental.pallas import tpu as pltpu
from jax.sharding import PartitionSpec as P

BS = 12
TAPS = 27
GY = 4
GZ = 2


NORM_EPSILON = 1e-06
OFFSETS = [(a, b, c) for a in (-1, 0, 1) for b in (-1, 0, 1) for c in (-1, 0, 1)]
DIRECTIONS = [
    item
    for level in (1, 2, 3)
    for item in OFFSETS
    if abs(item[0]) + abs(item[1]) + abs(item[2]) == level
]
COLUMNS = [(a, b) for a in (-1, 0, 1) for b in (-1, 0, 1)]


def side_range(component, edge):
    if component == 1:
        return (edge - 1, edge)
    if component == -1:
        return (0, 1)
    return (0, edge)


def halo_range(component, edge):
    if component == 1:
        return (edge + 1, edge + 2)
    if component == -1:
        return (0, 1)
    return (1, edge + 1)


def slab_count(direction, edge):
    total = 1
    for component in direction:
        total = total * (1 if component != 0 else edge)
    return total


def row_directions(edge, region_count):
    labels = []
    for position, direction in enumerate(DIRECTIONS):
        labels = labels + [position] * slab_count(direction, edge)
    per_peer = -(-len(labels) // region_count)
    labels = labels + [len(DIRECTIONS)] * (per_peer * region_count - len(labels))
    return (np.array(labels, dtype=np.int32).reshape(per_peer, region_count), len(labels), per_peer)


def holder_table(owner_row, region_count):
    slot_ids = jnp.arange(region_count, dtype=jnp.int32)
    block_of = jnp.sum(
        jnp.where(owner_row[None, :] == slot_ids[:, None], slot_ids[None, :], 0), axis=1
    )
    layer = GY * GZ
    across = region_count // layer
    block_x = block_of // layer
    block_y = block_of // GZ % GY
    block_z = block_of % GZ
    columns = []
    for direction in DIRECTIONS:
        near_x = block_x + direction[0]
        near_y = block_y + direction[1]
        near_z = block_z + direction[2]
        inside = (
            (near_x >= 0)
            & (near_x < across)
            & (near_y >= 0)
            & (near_y < GY)
            & (near_z >= 0)
            & (near_z < GZ)
        )
        target = jnp.clip(near_x * layer + near_y * GZ + near_z, 0, region_count - 1)
        holder = jnp.take(owner_row, target, axis=0)
        columns.append(jnp.where(inside, holder, -1))
    columns.append(jnp.full((region_count,), -1, jnp.int32))
    return jnp.stack(columns, axis=1)


def route_plan(owner_row, region_count):
    labels, padded_rows, per_peer = row_directions(BS, region_count)
    myself = lax.axis_index("region")
    labels_now = lax.dynamic_index_in_dim(jnp.asarray(labels), myself, 1, keepdims=False)
    holders = holder_table(owner_row, region_count)
    sources = jnp.take(holders, labels_now, axis=1)
    valid = sources >= 0
    positions = jnp.arange(per_peer, dtype=jnp.int32)[None, :]
    source_rows = jnp.where(valid, sources * per_peer + positions, 0).reshape(-1)
    return (source_rows, valid.astype(jnp.bfloat16), per_peer)


def dealt_shell(cube, region_count, per_peer):
    edge = cube.shape[0]
    width = cube.shape[3]
    pieces = []
    for direction in DIRECTIONS:
        spans = [side_range(-component, edge) for component in direction]
        pieces.append(
            cube[
                spans[0][0] : spans[0][1], spans[1][0] : spans[1][1], spans[2][0] : spans[2][1]
            ].reshape(-1, width)
        )
    rows = jnp.concatenate(pieces, axis=0)
    rows = jnp.pad(rows, ((0, per_peer * region_count - rows.shape[0]), (0, 0)))
    return rows.reshape(per_peer, region_count, width).transpose(1, 0, 2)


def pick_rows(holdings, plan):
    source_rows, valid, per_peer = plan
    width = holdings.shape[2]
    flat = holdings.reshape(-1, width)
    picked = jnp.take(flat, source_rows, axis=0).reshape(holdings.shape[0], per_peer, width)
    return picked * valid[..., None]


def relay(plan, cube, region_count):
    dealt = lax.all_to_all(
        dealt_shell(cube, region_count, plan[2]), "region", split_axis=0, concat_axis=0, tiled=True
    )
    return lax.all_to_all(pick_rows(dealt, plan), "region", split_axis=0, concat_axis=0, tiled=True)


def assemble(received, cube):
    edge = cube.shape[0]
    width = cube.shape[3]
    whole = received.transpose(1, 0, 2).reshape(-1, width)
    padded = jnp.pad(cube, ((1, 1), (1, 1), (1, 1), (0, 0)))
    offset = 0
    for direction in DIRECTIONS:
        spans = [halo_range(component, edge) for component in direction]
        lengths = [upper - lower for lower, upper in spans]
        count = lengths[0] * lengths[1] * lengths[2]
        piece = whole[offset : offset + count].reshape(lengths[0], lengths[1], lengths[2], width)
        padded = padded.at[
            spans[0][0] : spans[0][1], spans[1][0] : spans[1][1], spans[2][0] : spans[2][1]
        ].set(piece)
        offset = offset + count
    return padded


def column_window(padded, shift_x, shift_y, edge, width):
    column = padded[1 + shift_x : 1 + shift_x + edge, 1 + shift_y : 1 + shift_y + edge]
    return jnp.concatenate(
        [column[:, :, 1 + shift_z : 1 + shift_z + edge] for shift_z in (-1, 0, 1)], axis=-1
    ).reshape(-1, 3 * width)


def convolve(padded_act, padded_grad, grad_block, conv_weight):
    edge = padded_act.shape[0] - 2
    width = padded_act.shape[3]
    forward = jnp.zeros((edge * edge * edge, width), jnp.float32)
    backward = jnp.zeros((edge * edge * edge, width), jnp.float32)
    terms = []
    for group_index, (shift_x, shift_y) in enumerate(COLUMNS):
        group_weight = conv_weight[3 * group_index : 3 * group_index + 3]
        window = column_window(padded_act, shift_x, shift_y, edge, width)
        forward = forward + jnp.dot(
            window, group_weight.reshape(3 * width, width), preferred_element_type=jnp.float32
        )
        mirror_column = padded_grad[
            1 - shift_x : 1 - shift_x + edge, 1 - shift_y : 1 - shift_y + edge
        ]
        mirror = jnp.concatenate(
            [mirror_column[:, :, 1 - shift_z : 1 - shift_z + edge] for shift_z in (-1, 0, 1)],
            axis=-1,
        ).reshape(-1, 3 * width)
        backward = backward + jnp.dot(
            mirror,
            group_weight.transpose(0, 2, 1).reshape(3 * width, width),
            preferred_element_type=jnp.float32,
        )
        terms.append(
            lax.dot_general(
                window, grad_block, (((0,), (0,)), ((), ())), preferred_element_type=jnp.float32
            )
        )
    return (forward, backward, jnp.concatenate(terms, axis=0).reshape(TAPS, width, width))


def body(features, voxel_mask, cotangent, norm_gain, conv_weight, block_owner):
    width = features.shape[-1]
    region_count = lax.axis_size("region")
    plan = route_plan(block_owner[0], region_count)
    inputs = features[0, 0].astype(jnp.float32)
    mask_col = voxel_mask[0, 0].astype(jnp.float32)[:, None]
    rinv = lax.rsqrt(jnp.mean(inputs * inputs, axis=-1, keepdims=True) + NORM_EPSILON)
    normed = inputs * rinv
    pre = normed * norm_gain
    activity = (jax.nn.silu(pre) * mask_col).astype(jnp.bfloat16)
    grad_out = cotangent[0, 0] * voxel_mask[0, 0].astype(jnp.bfloat16)[:, None]
    act_cube = activity.reshape(BS, BS, BS, width)
    grad_cube = grad_out.reshape(BS, BS, BS, width)
    act_recv = relay(plan, act_cube, region_count)
    grad_recv = relay(plan, grad_cube, region_count)
    padded_act = assemble(act_recv, act_cube)
    padded_grad = assemble(grad_recv, grad_cube)
    forward, backward, weight_grad = convolve(padded_act, padded_grad, grad_out, conv_weight)
    block_output = (inputs + forward * mask_col).astype(jnp.bfloat16)
    slope = jax.nn.sigmoid(pre)
    dnorm = backward * mask_col * (slope * (1.0 + pre * (1.0 - slope))) * norm_gain
    dinput = rinv * (dnorm - normed * jnp.mean(dnorm * normed, axis=-1, keepdims=True))
    input_grad = (cotangent[0, 0].astype(jnp.float32) + dinput).astype(jnp.bfloat16)
    flat_grad = weight_grad.reshape(-1, width)
    share_rows = flat_grad.shape[0] // region_count
    limit = math.sqrt(flat_grad.shape[0] * width)
    summed = lax.psum(flat_grad, "region")
    total_squares = jnp.sum(summed * summed)
    share = lax.dynamic_slice_in_dim(summed, lax.axis_index("region") * share_rows, share_rows, 0)
    factor = jnp.minimum(1.0, limit / jnp.sqrt(total_squares))
    update = lax.psum(share * factor, "scene") / lax.axis_size("scene")
    return (block_output.reshape(features.shape), input_grad.reshape(cotangent.shape), update)


PLANE = BS * BS
ZPAD = 16
ROWS = BS * ZPAD
WIDE = (BS + 2) * ZPAD
EDGE_ROWS = 4 * BS
STACK = PLANE + EDGE_ROWS
PICKED = 16 * 7
GROUP = BS // 4
FACE_A, FACE_D, FACE_C, FACE_B = 0, BS, 2 * BS, 3 * BS


def extract_table():
    table = np.zeros((EDGE_ROWS, PLANE), np.float32)
    for i in range(BS):
        table[FACE_A + i, i] = 1
        table[FACE_D + i, i * BS + BS - 1] = 1
        table[FACE_C + i, i * BS] = 1
        table[FACE_B + i, (BS - 1) * BS + i] = 1
    return table


def compact_table():
    ym, yp, zn = 0, 16, 32
    ymz, ypz = zn + EDGE_ROWS, zn + EDGE_ROWS + 16
    table = np.zeros((GZ, EDGE_ROWS, PICKED), np.float32)
    for bz in range(GZ):
        near = 0 if bz == 0 else BS - 1
        for i in range(BS):
            table[bz, i, ym + FACE_B - 32 + i] = 1
            table[bz, BS + i, yp + FACE_A + i] = 1
            table[bz, 2 * BS + i, zn + (FACE_C if bz == 0 else FACE_D) + i] = 1
        table[bz, 3 * BS, ymz + FACE_B - 32 + near] = 1
        table[bz, 3 * BS + 1, ypz + FACE_A + near] = 1
    return table


def spread_table():
    table = np.zeros((GZ, 3, BS + 2, ZPAD, STACK), np.float32)
    for bz in range(GZ):
        for c in range(3):
            for y in range(-1, BS + 1):
                for row in range(BS + 2):
                    z = row - 1 + c - 1
                    if z < -1 or z > BS:
                        continue
                    y_in, z_in = 0 <= y < BS, 0 <= z < BS
                    if not z_in and (z < 0) != (bz == 1):
                        continue
                    if y_in and z_in:
                        col = y * BS + z
                    elif z_in:
                        col = PLANE + z if y < 0 else PLANE + BS + z
                    elif y_in:
                        col = PLANE + 2 * BS + y
                    else:
                        col = PLANE + 3 * BS if y < 0 else PLANE + 3 * BS + 1
                    table[bz, c, y + 1, row, col] = 1
    return table


def fused_kernel(
    feat_h, cot_h, weight_h, extract_h, compact_h, own_spread_h, spread_h, squeeze_h, mask, gain, owner,
    out, grad_in, update,
    feat, cot, weight, extract, compact, own_spread, spread, squeeze,
    g_msg, a_msg, deal, deliver, halo, g_stack, a_stack, g_wide, a_wide, own_wide, own_turned,
    normed_s, slope_s, rinv_s, part, from_twin, pair16, pair_own, from_z, squares, shares, factors,
    load_sem, deal_send, deal_recv, halo_send, halo_recv,
    twin_send, twin_recv, z_send, z_recv, sq_send, sq_recv, sh_send, sh_recv, fa_send, fa_recv,
):
    f32, bf16 = jnp.float32, jnp.bfloat16
    me = lax.axis_index("region")
    scene = lax.axis_index("scene")
    core = lax.rem(me, 2)
    chip = lax.div(me, 2)
    chips = GY * GZ // 2
    twin = 2 * chip + 1 - core
    share_rows = TAPS * 128 // (GY * GZ)

    def remote(src, dst, send, recv, **where):
        return pltpu.make_async_remote_copy(
            src_ref=src, dst_ref=dst, send_sem=send, recv_sem=recv,
            device_id=where, device_id_type=pl.DeviceIdType.MESH,
        )

    loads = [
        pltpu.make_async_copy(src, dst, load_sem.at[i])
        for i, (src, dst) in enumerate(
            (
                (cot_h, cot), (extract_h, extract), (feat_h, feat), (compact_h, compact),
                (own_spread_h, own_spread), (spread_h, spread), (weight_h, weight), (squeeze_h, squeeze),
            )
        )
    ]
    for load in loads:
        load.start()
    barrier = pltpu.get_barrier_semaphore()
    for k in range(1, 8):
        pl.semaphore_signal(barrier, inc=1, device_id={"region": lax.rem(me + k, 8)}, device_id_type=pl.DeviceIdType.MESH)
    for k in range(1, 4):
        pl.semaphore_signal(barrier, inc=1, device_id={"scene": lax.rem(scene + k, 4)}, device_id_type=pl.DeviceIdType.MESH)

    def at_plane(x, step):
        return pl.ds(pl.multiple_of(x * step, step), step)

    def neighbours(slot):
        block = jnp.int32(0)
        for k in range(1, GY * GZ):
            block = block + jnp.where(owner[0, k] == slot, k, 0)
        by, bz = lax.div(block, GZ), lax.rem(block, GZ)

        def holder(y, z):
            held = owner[0, jnp.clip(y * GZ + z, 0, GY * GZ - 1)]
            return jnp.where((y >= 0) & (y < GY), held, GY * GZ)

        return (
            holder(by - 1, bz), holder(by + 1, bz), holder(by, 1 - bz),
            holder(by - 1, 1 - bz), holder(by + 1, 1 - bz), bz,
        )

    def grad_plane(x, carry):
        rows = at_plane(x, PLANE)
        g = cot[rows, :] * mask[rows, :]
        g_stack[x, 0:PLANE, :] = g
        g_msg[at_plane(x, EDGE_ROWS), :] = jnp.dot(extract[...], g, preferred_element_type=f32).astype(bf16)
        return carry

    loads[0].wait()
    loads[1].wait()
    lax.fori_loop(0, BS, grad_plane, 0, unroll=2)
    pl.semaphore_wait(barrier, 10)

    deal_rows = GROUP * EDGE_ROWS

    def deal_copy(which, msg, k):
        q = lax.rem(chip + k, chips)
        return remote(
            msg.at[at_plane(q, deal_rows)], deal.at[me], deal_send.at[which, k], deal_recv.at[me], region=2 * q + which
        )

    def start_deal(which, msg):
        for k in (2, 1, 3):
            deal_copy(which, msg, k).start()

        @pl.when(core != which)
        def _():
            deal_copy(which, msg, 0).start()

        @pl.when(core == which)
        def _():
            deal[me] = msg[at_plane(chip, deal_rows), :]

    def deal_arrival(slot):
        return remote(deal.at[slot], deal.at[slot], deal_send.at[0, 0], deal_recv.at[slot], region=twin)

    def halo_copy(k):
        slot = lax.rem(me + k, 8)
        return remote(
            deliver.at[slot], halo.at[core, at_plane(chip, deal_rows)], halo_send.at[k - 1], halo_recv.at[core, chip], region=slot
        )

    def halo_arrival(which, q):
        rows = halo.at[which, at_plane(q, deal_rows)]
        return remote(rows, rows, halo_send.at[0], halo_recv.at[which, q], region=twin)

    def end_halo(which):
        for k in (1, 3, 2):
            halo_arrival(which, lax.rem(chip + k, chips)).wait_recv()

        @pl.when(core != which)
        def _():
            halo_arrival(which, chip).wait_recv()

    start_deal(0, g_msg)
    deal[8] = jnp.zeros(deal.shape[1:], bf16)
    loads[2].wait()

    def act_plane(x, carry):
        rows = at_plane(x, PLANE)
        inputs = feat[rows, :].astype(f32)
        rinv = lax.rsqrt(jnp.mean(inputs * inputs, axis=-1, keepdims=True) + NORM_EPSILON)
        normed = inputs * rinv
        pre = normed * gain[...]
        slope = 1.0 / (1.0 + jnp.exp(-pre))
        kept = mask[rows, :].astype(f32)
        act = (pre * slope * kept).astype(bf16)
        normed_s[rows, :] = normed
        slope_s[rows, :] = kept * (slope * (1.0 + pre * (1.0 - slope))) * gain[...]
        rinv_s[rows, :] = jnp.broadcast_to(rinv, normed.shape)
        a_stack[x, 0:PLANE, :] = act
        a_msg[at_plane(x, EDGE_ROWS), :] = jnp.dot(extract[...], act, preferred_element_type=f32).astype(bf16)
        return carry

    lax.fori_loop(0, BS, act_plane, 0, unroll=2)
    start_deal(1, a_msg)
    loads[3].wait()
    for k in range(1, 8):
        deal_arrival(lax.rem(me + k, 8)).wait_recv()

    def pick_for(slot):
        ym, yp, zn, ymz, ypz, bz = neighbours(slot)
        picked = []
        for p in range(GROUP):
            first = p * EDGE_ROWS
            low, high = slice(first, first + 16), slice(first + 32, first + 48)
            rows = jnp.concatenate(
                [deal[ym, high, :], deal[yp, low, :], deal[zn, first : first + EDGE_ROWS, :], deal[ymz, high, :], deal[ypz, low, :]],
                axis=0,
            )
            picked.append(jnp.dot(compact[bz], rows, preferred_element_type=f32).astype(bf16))
        return jnp.concatenate(picked, axis=0)

    for k in (4, 5, 3, 2, 6, 7, 1):
        slot = lax.rem(me + k, 8)
        deliver[slot] = pick_for(slot)
        halo_copy(k).start()
    halo[core, at_plane(chip, deal_rows), :] = pick_for(me)
    my_height = neighbours(me)[5]
    loads[4].wait()

    def own_plane(x, carry):
        moved = jnp.dot(own_spread[...], a_stack[x, 0:PLANE, :], preferred_element_type=f32).astype(bf16)
        for c in range(3):
            own_wide[at_plane(x, ROWS), c * 128 : (c + 1) * 128] = moved[c * ROWS : (c + 1) * ROWS]
        return carry

    lax.fori_loop(0, BS, own_plane, 0, unroll=2)
    turn = 4 * ROWS
    for i in range(3):
        for c in range(3):
            own_turned[c * 128 : (c + 1) * 128, i * turn : (i + 1) * turn] = own_wide[
                i * turn : (i + 1) * turn, c * 128 : (c + 1) * 128
            ].T

    def widen(which, stack, wide):
        wide[0] = jnp.zeros(wide.shape[1:], bf16)
        wide[BS + 1] = jnp.zeros(wide.shape[1:], bf16)

        def plane(x, carry):
            stack[x, PLANE:STACK, :] = halo[which, at_plane(x, EDGE_ROWS), :]
            moved = jnp.dot(spread[my_height], stack[x], preferred_element_type=f32).astype(bf16)
            for c in range(3):
                wide[x + 1, :, c * 128 : (c + 1) * 128] = moved[c * WIDE : (c + 1) * WIDE]
            return carry

        lax.fori_loop(0, BS, plane, 0, unroll=2)

    loads[5].wait()
    end_halo(0)
    widen(0, g_stack, g_wide)

    def window(a, b):
        return g_wide[1 - a : 1 - a + BS, (1 - b) * ZPAD : (1 - b) * ZPAD + ROWS, 128:256].reshape(BS * ROWS, 128)

    for first in range(0, 9, 2):
        group = list(range(first, min(first + 2, 9)))
        side = [window(*COLUMNS[i]) for i in group]
        rhs = jnp.concatenate(side, axis=1) if len(side) > 1 else side[0]
        term = jnp.dot(own_turned[...], rhs, preferred_element_type=f32)
        for j, i in enumerate(group):
            part[3 * i * 128 : (3 * i + 3) * 128, :] = term[:, j * 128 : (j + 1) * 128]

    def share_of(index):
        return pl.ds(pl.multiple_of(index * share_rows, 16), share_rows)

    def twin_copy(q):
        return remote(part.at[share_of(2 * q + 1 - core)], from_twin.at[q], twin_send.at[q], twin_recv.at[q], region=twin)

    for q in range(chips):
        twin_copy(q).start()

    def z_copy(k):
        target = lax.rem(chip + k, chips)
        return remote(pair16.at[target], from_z.at[k - 1], z_send.at[k - 1], z_recv.at[k - 1], region=2 * target + core)

    for q in range(chips):
        twin_copy(q).wait_recv()
    for k in (2, 1, 3):
        q = lax.rem(chip + k, chips)
        pair16[q] = (part[share_of(2 * q + core), :] + from_twin[q]).astype(bf16)
        z_copy(k).start()
    pair_own[...] = part[share_of(me), :] + from_twin[chip]

    count = 3

    def convolve_planes(wide, taps, x0, transposed):
        total = None
        for a in range(3):
            lhs = jnp.concatenate(
                [wide[pl.ds(x0 + a, count), b * ZPAD : b * ZPAD + ROWS, :].reshape(count * ROWS, 384) for b in range(3)],
                axis=1,
            )
            if transposed:
                rhs = jnp.concatenate([taps[26 - 9 * a - j] for j in range(9)], axis=1)
                term = lax.dot_general(lhs, rhs, (((1,), (1,)), ((), ())), preferred_element_type=f32)
            else:
                term = jnp.dot(lhs, taps[9 * a : 9 * a + 9].reshape(9 * 128, 128), preferred_element_type=f32)
            total = term if total is None else total + term
        planes = []
        for i in range(count):
            piece = total[i * ROWS : (i + 1) * ROWS]
            high = piece.astype(bf16)
            rest = (piece - high.astype(f32)).astype(bf16)
            planes.append(jnp.dot(squeeze[...], jnp.concatenate([high, rest], axis=0), preferred_element_type=f32))
        return planes

    def backward_planes(step, carry):
        x0 = step * count
        for i, back in enumerate(convolve_planes(g_wide, weight, x0, True)):
            rows = at_plane(x0 + i, PLANE)
            normed = normed_s[rows, :]
            dnorm = back * slope_s[rows, :]
            level = jnp.mean(dnorm * normed, axis=-1, keepdims=True)
            grad_in[rows, :] = (cot[rows, :].astype(f32) + rinv_s[rows, :] * (dnorm - normed * level)).astype(bf16)
        return carry

    loads[6].wait()
    loads[7].wait()
    lax.fori_loop(0, BS // count, backward_planes, 0)

    end_halo(1)
    widen(1, a_stack, a_wide)

    def z_wait(k):
        z_copy(k).wait_recv()

    for k in (1, 3, 2):
        z_wait(k)
    share = pair_own[...] + from_z[0].astype(f32) + from_z[1].astype(f32) + from_z[2].astype(f32)
    squares[me] = jnp.sum((share * share).reshape(share_rows // 8, 8, 128), axis=0)
    shares[scene] = share.astype(bf16)

    def sq_copy(k):
        return remote(squares.at[me], squares.at[me], sq_send.at[k - 1], sq_recv.at[k - 1], region=lax.rem(me + k, 8))

    def sq_arrival(k):
        slot = lax.rem(me + 8 - k, 8)
        return remote(squares.at[slot], squares.at[slot], sq_send.at[k - 1], sq_recv.at[k - 1], region=slot)

    def scene_copy(buf, send, recv, k):
        return remote(buf.at[scene], buf.at[scene], send.at[k - 1], recv.at[k - 1], scene=lax.rem(scene + k, 4))

    def scene_arrival(buf, send, recv, k):
        slot = lax.rem(scene + 4 - k, 4)
        return remote(buf.at[slot], buf.at[slot], send.at[k - 1], recv.at[k - 1], scene=slot)

    for k in range(1, 8):
        sq_copy(k).start()
    for k in range(1, 4):
        scene_copy(shares, sh_send, sh_recv, k).start()

    def forward_planes(step, carry):
        x0 = step * count
        for i, ahead in enumerate(convolve_planes(a_wide, weight, x0, False)):
            rows = at_plane(x0 + i, PLANE)
            out[rows, :] = (feat[rows, :].astype(f32) + ahead * mask[rows, :].astype(f32)).astype(bf16)
        return carry

    lax.fori_loop(0, 1, forward_planes, 0)
    for k in range(1, 8):
        sq_arrival(k).wait_recv()
    total = jnp.sum(jnp.sum(squares[...], axis=0), keepdims=True)
    limit = math.sqrt(TAPS * 128 * 128)
    factors[scene] = jnp.broadcast_to(jnp.minimum(1.0, limit * lax.rsqrt(total)), (8, 128))
    for k in range(1, 4):
        scene_copy(factors, fa_send, fa_recv, k).start()
    lax.fori_loop(1, BS // count, forward_planes, 0)
    for k in range(1, 4):
        scene_arrival(shares, sh_send, sh_recv, k).wait_recv()
        scene_arrival(factors, fa_send, fa_recv, k).wait_recv()
    result = jnp.zeros((share_rows, 128), f32)
    for s in range(4):
        result = result + factors[s, 0:1, :] * shares[s].astype(f32)
    update[...] = result * 0.25

    for which, msg in ((0, g_msg), (1, a_msg)):
        for k in range(1, 4):
            deal_copy(which, msg, k).wait_send()
    for which, msg in ((0, g_msg), (1, a_msg)):

        @pl.when(core != which)
        def _(which=which, msg=msg):
            deal_copy(which, msg, 0).wait_send()

    for k in range(1, 8):
        halo_copy(k).wait_send()
    for q in range(chips):
        twin_copy(q).wait_send()
    for k in range(1, 4):
        z_copy(k).wait_send()
        scene_copy(shares, sh_send, sh_recv, k).wait_send()
        scene_copy(factors, fa_send, fa_recv, k).wait_send()
    for k in range(1, 8):
        sq_copy(k).wait_send()


def fused_body(features, voxel_mask, cotangent, norm_gain, conv_weight, block_owner):
    f32, bf16 = jnp.float32, jnp.bfloat16
    width = features.shape[-1]
    slots = lax.axis_size("region")
    spread = spread_table()
    own = spread[0, :, 1 : 1 + BS, :, :PLANE].reshape(3 * ROWS, PLANE)
    squeeze = np.zeros((BS, BS, BS, ZPAD), np.float32)
    for y in range(BS):
        for z in range(BS):
            squeeze[y, z, y, z + 1] = 1
    squeeze = squeeze.reshape(PLANE, ROWS)
    squeeze = np.concatenate([squeeze, squeeze], axis=1)
    spread = spread.reshape(GZ, 3 * WIDE, STACK)
    voxels = BS * BS * BS
    mask = jnp.broadcast_to(voxel_mask[0, 0].astype(bf16)[:, None], (voxels, width))
    vmem = pl.BlockSpec(memory_space=pltpu.VMEM)
    share_rows = TAPS * width // slots
    sem = pltpu.SemaphoreType.DMA
    tables = [jnp.asarray(table, bf16) for table in (extract_table(), compact_table(), own, spread, squeeze)]
    hbm = [features[0, 0], cotangent[0, 0], conv_weight, *tables]
    out, grad_in, update = pl.pallas_call(
        fused_kernel,
        out_shape=(
            jax.ShapeDtypeStruct((voxels, width), bf16),
            jax.ShapeDtypeStruct((voxels, width), bf16),
            jax.ShapeDtypeStruct((share_rows, width), f32),
        ),
        in_specs=[pl.BlockSpec(memory_space=pltpu.HBM)] * 8 + [vmem, vmem, pl.BlockSpec(memory_space=pltpu.SMEM)],
        out_specs=(vmem, vmem, vmem),
        scratch_shapes=[
            *[pltpu.VMEM(table.shape, bf16) for table in hbm],
            pltpu.VMEM((BS * EDGE_ROWS, width), bf16),
            pltpu.VMEM((BS * EDGE_ROWS, width), bf16),
            pltpu.VMEM((slots + 1, GROUP * EDGE_ROWS, width), bf16),
            pltpu.VMEM((slots, GROUP * EDGE_ROWS, width), bf16),
            pltpu.VMEM((2, BS * EDGE_ROWS, width), bf16),
            pltpu.VMEM((BS, STACK, width), bf16),
            pltpu.VMEM((BS, STACK, width), bf16),
            pltpu.VMEM((BS + 2, WIDE, 3 * width), bf16),
            pltpu.VMEM((BS + 2, WIDE, 3 * width), bf16),
            pltpu.VMEM((BS * ROWS, 3 * width), bf16),
            pltpu.VMEM((3 * width, BS * ROWS), bf16),
            pltpu.VMEM((voxels, width), f32),
            pltpu.VMEM((voxels, width), f32),
            pltpu.VMEM((voxels, width), f32),
            pltpu.VMEM((TAPS * width, width), f32),
            pltpu.VMEM((slots // 2, share_rows, width), f32),
            pltpu.VMEM((slots // 2, share_rows, width), bf16),
            pltpu.VMEM((share_rows, width), f32),
            pltpu.VMEM((slots // 2 - 1, share_rows, width), bf16),
            pltpu.VMEM((slots, 8, width), f32),
            pltpu.VMEM((4, share_rows, width), bf16),
            pltpu.VMEM((4, 8, width), f32),
            sem((8,)),
            sem((2, 4)), sem((slots,)),
            sem((7,)), sem((2, slots // 2)),
            sem((slots // 2,)), sem((slots // 2,)),
            sem((3,)), sem((3,)),
            sem((7,)), sem((7,)),
            sem((3,)), sem((3,)),
            sem((3,)), sem((3,)),
        ],
        compiler_params=pltpu.CompilerParams(
            collective_id=0, has_side_effects=True, vmem_limit_bytes=50 * 1024 * 1024
        ),
        cost_estimate=pl.CostEstimate(flops=5_000_000_000, bytes_accessed=4_000_000, transcendentals=300_000),
    )(
        *hbm, mask, norm_gain[None, :], block_owner,
    )
    return (out.reshape(features.shape), grad_in.reshape(cotangent.shape), update)


def solution(mesh):
    in_specs = (
        P("scene", "region", None, None),
        P("scene", "region", None),
        P("scene", "region", None, None),
        P(),
        P(),
        P("scene", None),
    )
    out_specs = (
        P("scene", "region", None, None),
        P("scene", "region", None, None),
        P("region", None),
    )
    chosen = fused_body if mesh.shape["region"] == GY * GZ else body
    return jax.shard_map(chosen, mesh=mesh, in_specs=in_specs, out_specs=out_specs, check_vma=False)
```

```python
import functools
import math

import jax
import jax.numpy as jnp
import numpy as np
from jax import lax
from jax.experimental import pallas as pl
from jax.experimental.pallas import tpu as pltpu
from jax.sharding import PartitionSpec as P

BS = 12
TAPS = 27
GY = 4
GZ = 2


NORM_EPSILON = 1e-06
OFFSETS = [(a, b, c) for a in (-1, 0, 1) for b in (-1, 0, 1) for c in (-1, 0, 1)]
DIRECTIONS = [
    item
    for level in (1, 2, 3)
    for item in OFFSETS
    if abs(item[0]) + abs(item[1]) + abs(item[2]) == level
]
COLUMNS = [(a, b) for a in (-1, 0, 1) for b in (-1, 0, 1)]


def side_range(component, edge):
    if component == 1:
        return (edge - 1, edge)
    if component == -1:
        return (0, 1)
    return (0, edge)


def halo_range(component, edge):
    if component == 1:
        return (edge + 1, edge + 2)
    if component == -1:
        return (0, 1)
    return (1, edge + 1)


def slab_count(direction, edge):
    total = 1
    for component in direction:
        total = total * (1 if component != 0 else edge)
    return total


def row_directions(edge, region_count):
    labels = []
    for position, direction in enumerate(DIRECTIONS):
        labels = labels + [position] * slab_count(direction, edge)
    per_peer = -(-len(labels) // region_count)
    labels = labels + [len(DIRECTIONS)] * (per_peer * region_count - len(labels))
    return (np.array(labels, dtype=np.int32).reshape(per_peer, region_count), len(labels), per_peer)


def holder_table(owner_row, region_count):
    slot_ids = jnp.arange(region_count, dtype=jnp.int32)
    block_of = jnp.sum(
        jnp.where(owner_row[None, :] == slot_ids[:, None], slot_ids[None, :], 0), axis=1
    )
    layer = GY * GZ
    across = region_count // layer
    block_x = block_of // layer
    block_y = block_of // GZ % GY
    block_z = block_of % GZ
    columns = []
    for direction in DIRECTIONS:
        near_x = block_x + direction[0]
        near_y = block_y + direction[1]
        near_z = block_z + direction[2]
        inside = (
            (near_x >= 0)
            & (near_x < across)
            & (near_y >= 0)
            & (near_y < GY)
            & (near_z >= 0)
            & (near_z < GZ)
        )
        target = jnp.clip(near_x * layer + near_y * GZ + near_z, 0, region_count - 1)
        holder = jnp.take(owner_row, target, axis=0)
        columns.append(jnp.where(inside, holder, -1))
    columns.append(jnp.full((region_count,), -1, jnp.int32))
    return jnp.stack(columns, axis=1)


def route_plan(owner_row, region_count):
    labels, padded_rows, per_peer = row_directions(BS, region_count)
    myself = lax.axis_index("region")
    labels_now = lax.dynamic_index_in_dim(jnp.asarray(labels), myself, 1, keepdims=False)
    holders = holder_table(owner_row, region_count)
    sources = jnp.take(holders, labels_now, axis=1)
    valid = sources >= 0
    positions = jnp.arange(per_peer, dtype=jnp.int32)[None, :]
    source_rows = jnp.where(valid, sources * per_peer + positions, 0).reshape(-1)
    return (source_rows, valid.astype(jnp.bfloat16), per_peer)


def dealt_shell(cube, region_count, per_peer):
    edge = cube.shape[0]
    width = cube.shape[3]
    pieces = []
    for direction in DIRECTIONS:
        spans = [side_range(-component, edge) for component in direction]
        pieces.append(
            cube[
                spans[0][0] : spans[0][1], spans[1][0] : spans[1][1], spans[2][0] : spans[2][1]
            ].reshape(-1, width)
        )
    rows = jnp.concatenate(pieces, axis=0)
    rows = jnp.pad(rows, ((0, per_peer * region_count - rows.shape[0]), (0, 0)))
    return rows.reshape(per_peer, region_count, width).transpose(1, 0, 2)


def pick_rows(holdings, plan):
    source_rows, valid, per_peer = plan
    width = holdings.shape[2]
    flat = holdings.reshape(-1, width)
    picked = jnp.take(flat, source_rows, axis=0).reshape(holdings.shape[0], per_peer, width)
    return picked * valid[..., None]


def relay(plan, cube, region_count):
    dealt = lax.all_to_all(
        dealt_shell(cube, region_count, plan[2]), "region", split_axis=0, concat_axis=0, tiled=True
    )
    return lax.all_to_all(pick_rows(dealt, plan), "region", split_axis=0, concat_axis=0, tiled=True)


def assemble(received, cube):
    edge = cube.shape[0]
    width = cube.shape[3]
    whole = received.transpose(1, 0, 2).reshape(-1, width)
    padded = jnp.pad(cube, ((1, 1), (1, 1), (1, 1), (0, 0)))
    offset = 0
    for direction in DIRECTIONS:
        spans = [halo_range(component, edge) for component in direction]
        lengths = [upper - lower for lower, upper in spans]
        count = lengths[0] * lengths[1] * lengths[2]
        piece = whole[offset : offset + count].reshape(lengths[0], lengths[1], lengths[2], width)
        padded = padded.at[
            spans[0][0] : spans[0][1], spans[1][0] : spans[1][1], spans[2][0] : spans[2][1]
        ].set(piece)
        offset = offset + count
    return padded


def column_window(padded, shift_x, shift_y, edge, width):
    column = padded[1 + shift_x : 1 + shift_x + edge, 1 + shift_y : 1 + shift_y + edge]
    return jnp.concatenate(
        [column[:, :, 1 + shift_z : 1 + shift_z + edge] for shift_z in (-1, 0, 1)], axis=-1
    ).reshape(-1, 3 * width)


def convolve(padded_act, padded_grad, grad_block, conv_weight):
    edge = padded_act.shape[0] - 2
    width = padded_act.shape[3]
    forward = jnp.zeros((edge * edge * edge, width), jnp.float32)
    backward = jnp.zeros((edge * edge * edge, width), jnp.float32)
    terms = []
    for group_index, (shift_x, shift_y) in enumerate(COLUMNS):
        group_weight = conv_weight[3 * group_index : 3 * group_index + 3]
        window = column_window(padded_act, shift_x, shift_y, edge, width)
        forward = forward + jnp.dot(
            window, group_weight.reshape(3 * width, width), preferred_element_type=jnp.float32
        )
        mirror_column = padded_grad[
            1 - shift_x : 1 - shift_x + edge, 1 - shift_y : 1 - shift_y + edge
        ]
        mirror = jnp.concatenate(
            [mirror_column[:, :, 1 - shift_z : 1 - shift_z + edge] for shift_z in (-1, 0, 1)],
            axis=-1,
        ).reshape(-1, 3 * width)
        backward = backward + jnp.dot(
            mirror,
            group_weight.transpose(0, 2, 1).reshape(3 * width, width),
            preferred_element_type=jnp.float32,
        )
        terms.append(
            lax.dot_general(
                window, grad_block, (((0,), (0,)), ((), ())), preferred_element_type=jnp.float32
            )
        )
    return (forward, backward, jnp.concatenate(terms, axis=0).reshape(TAPS, width, width))


def body(features, voxel_mask, cotangent, norm_gain, conv_weight, block_owner):
    width = features.shape[-1]
    region_count = lax.axis_size("region")
    plan = route_plan(block_owner[0], region_count)
    inputs = features[0, 0].astype(jnp.float32)
    mask_col = voxel_mask[0, 0].astype(jnp.float32)[:, None]
    rinv = lax.rsqrt(jnp.mean(inputs * inputs, axis=-1, keepdims=True) + NORM_EPSILON)
    normed = inputs * rinv
    pre = normed * norm_gain
    activity = (jax.nn.silu(pre) * mask_col).astype(jnp.bfloat16)
    grad_out = cotangent[0, 0] * voxel_mask[0, 0].astype(jnp.bfloat16)[:, None]
    act_cube = activity.reshape(BS, BS, BS, width)
    grad_cube = grad_out.reshape(BS, BS, BS, width)
    act_recv = relay(plan, act_cube, region_count)
    grad_recv = relay(plan, grad_cube, region_count)
    padded_act = assemble(act_recv, act_cube)
    padded_grad = assemble(grad_recv, grad_cube)
    forward, backward, weight_grad = convolve(padded_act, padded_grad, grad_out, conv_weight)
    block_output = (inputs + forward * mask_col).astype(jnp.bfloat16)
    slope = jax.nn.sigmoid(pre)
    dnorm = backward * mask_col * (slope * (1.0 + pre * (1.0 - slope))) * norm_gain
    dinput = rinv * (dnorm - normed * jnp.mean(dnorm * normed, axis=-1, keepdims=True))
    input_grad = (cotangent[0, 0].astype(jnp.float32) + dinput).astype(jnp.bfloat16)
    flat_grad = weight_grad.reshape(-1, width)
    share_rows = flat_grad.shape[0] // region_count
    limit = math.sqrt(flat_grad.shape[0] * width)
    summed = lax.psum(flat_grad, "region")
    total_squares = jnp.sum(summed * summed)
    share = lax.dynamic_slice_in_dim(summed, lax.axis_index("region") * share_rows, share_rows, 0)
    factor = jnp.minimum(1.0, limit / jnp.sqrt(total_squares))
    update = lax.psum(share * factor, "scene") / lax.axis_size("scene")
    return (block_output.reshape(features.shape), input_grad.reshape(cotangent.shape), update)


PLANE = BS * BS
ZPAD = 16
ROWS = BS * ZPAD
WIDE = (BS + 2) * ZPAD
EDGE_ROWS = 4 * BS
STACK = PLANE + EDGE_ROWS
PICKED = 16 * 7
GROUP = BS // 4
FACE_A, FACE_D, FACE_C, FACE_B = 0, BS, 2 * BS, 3 * BS


def extract_table():
    table = np.zeros((EDGE_ROWS, PLANE), np.float32)
    for i in range(BS):
        table[FACE_A + i, i] = 1
        table[FACE_D + i, i * BS + BS - 1] = 1
        table[FACE_C + i, i * BS] = 1
        table[FACE_B + i, (BS - 1) * BS + i] = 1
    return table


def compact_table():
    ym, yp, zn = 0, 16, 32
    ymz, ypz = zn + EDGE_ROWS, zn + EDGE_ROWS + 16
    table = np.zeros((GZ, EDGE_ROWS, PICKED), np.float32)
    for bz in range(GZ):
        near = 0 if bz == 0 else BS - 1
        for i in range(BS):
            table[bz, i, ym + FACE_B - 32 + i] = 1
            table[bz, BS + i, yp + FACE_A + i] = 1
            table[bz, 2 * BS + i, zn + (FACE_C if bz == 0 else FACE_D) + i] = 1
        table[bz, 3 * BS, ymz + FACE_B - 32 + near] = 1
        table[bz, 3 * BS + 1, ypz + FACE_A + near] = 1
    return table


def spread_table():
    table = np.zeros((GZ, 3, BS + 2, ZPAD, STACK), np.float32)
    for bz in range(GZ):
        for c in range(3):
            for y in range(-1, BS + 1):
                for row in range(BS + 2):
                    z = row - 1 + c - 1
                    if z < -1 or z > BS:
                        continue
                    y_in, z_in = 0 <= y < BS, 0 <= z < BS
                    if not z_in and (z < 0) != (bz == 1):
                        continue
                    if y_in and z_in:
                        col = y * BS + z
                    elif z_in:
                        col = PLANE + z if y < 0 else PLANE + BS + z
                    elif y_in:
                        col = PLANE + 2 * BS + y
                    else:
                        col = PLANE + 3 * BS if y < 0 else PLANE + 3 * BS + 1
                    table[bz, c, y + 1, row, col] = 1
    return table


def fused_kernel(
    feat_h, cot_h, weight_h, extract_h, compact_h, own_spread_h, spread_h, squeeze_h, mask, gain, owner,
    out, grad_in, update,
    feat, cot, weight, extract, compact, own_spread, spread, squeeze,
    g_msg, a_msg, deal, deliver, halo, g_stack, a_stack, g_wide, a_wide, own_wide, own_turned,
    normed_s, slope_s, rinv_s, part, from_twin, pair16, pair_own, from_z, squares, shares, factors,
    load_sem, deal_send, deal_recv, halo_send, halo_recv,
    twin_send, twin_recv, z_send, z_recv, sq_send, sq_recv, sh_send, sh_recv, fa_send, fa_recv,
):
    f32, bf16 = jnp.float32, jnp.bfloat16
    me = lax.axis_index("region")
    scene = lax.axis_index("scene")
    core = lax.rem(me, 2)
    chip = lax.div(me, 2)
    chips = GY * GZ // 2
    twin = 2 * chip + 1 - core
    share_rows = TAPS * 128 // (GY * GZ)

    def remote(src, dst, send, recv, **where):
        return pltpu.make_async_remote_copy(
            src_ref=src, dst_ref=dst, send_sem=send, recv_sem=recv,
            device_id=where, device_id_type=pl.DeviceIdType.MESH,
        )

    loads = [
        pltpu.make_async_copy(src, dst, load_sem.at[i])
        for i, (src, dst) in enumerate(
            (
                (cot_h, cot), (extract_h, extract), (feat_h, feat), (compact_h, compact),
                (own_spread_h, own_spread), (spread_h, spread), (weight_h, weight), (squeeze_h, squeeze),
            )
        )
    ]
    for load in loads:
        load.start()
    barrier = pltpu.get_barrier_semaphore()
    for k in range(1, 8):
        pl.semaphore_signal(barrier, inc=1, device_id={"region": lax.rem(me + k, 8)}, device_id_type=pl.DeviceIdType.MESH)
    for k in range(1, 4):
        pl.semaphore_signal(barrier, inc=1, device_id={"scene": lax.rem(scene + k, 4)}, device_id_type=pl.DeviceIdType.MESH)

    def at_plane(x, step):
        return pl.ds(pl.multiple_of(x * step, step), step)

    def neighbours(slot):
        block = jnp.int32(0)
        for k in range(1, GY * GZ):
            block = block + jnp.where(owner[0, k] == slot, k, 0)
        by, bz = lax.div(block, GZ), lax.rem(block, GZ)

        def holder(y, z):
            held = owner[0, jnp.clip(y * GZ + z, 0, GY * GZ - 1)]
            return jnp.where((y >= 0) & (y < GY), held, GY * GZ)

        return (
            holder(by - 1, bz), holder(by + 1, bz), holder(by, 1 - bz),
            holder(by - 1, 1 - bz), holder(by + 1, 1 - bz), bz,
        )

    def grad_plane(x, carry):
        rows = at_plane(x, PLANE)
        g = cot[rows, :] * mask[rows, :]
        g_stack[x, 0:PLANE, :] = g
        g_msg[at_plane(x, EDGE_ROWS), :] = jnp.dot(extract[...], g, preferred_element_type=f32).astype(bf16)
        return carry

    loads[0].wait()
    loads[1].wait()
    lax.fori_loop(0, BS, grad_plane, 0, unroll=2)
    pl.semaphore_wait(barrier, 10)

    deal_rows = GROUP * EDGE_ROWS

    def deal_copy(which, msg, k):
        q = lax.rem(chip + k, chips)
        return remote(
            msg.at[at_plane(q, deal_rows)], deal.at[me], deal_send.at[which, k], deal_recv.at[me], region=2 * q + which
        )

    def start_deal(which, msg):
        for k in (2, 1, 3):
            deal_copy(which, msg, k).start()

        @pl.when(core != which)
        def _():
            deal_copy(which, msg, 0).start()

        @pl.when(core == which)
        def _():
            deal[me] = msg[at_plane(chip, deal_rows), :]

    def deal_arrival(slot):
        return remote(deal.at[slot], deal.at[slot], deal_send.at[0, 0], deal_recv.at[slot], region=twin)

    def halo_copy(k):
        slot = lax.rem(me + k, 8)
        return remote(
            deliver.at[slot], halo.at[core, at_plane(chip, deal_rows)], halo_send.at[k - 1], halo_recv.at[core, chip], region=slot
        )

    def halo_arrival(which, q):
        rows = halo.at[which, at_plane(q, deal_rows)]
        return remote(rows, rows, halo_send.at[0], halo_recv.at[which, q], region=twin)

    def end_halo(which):
        for k in (1, 3, 2):
            halo_arrival(which, lax.rem(chip + k, chips)).wait_recv()

        @pl.when(core != which)
        def _():
            halo_arrival(which, chip).wait_recv()

    start_deal(0, g_msg)
    deal[8] = jnp.zeros(deal.shape[1:], bf16)
    loads[2].wait()

    def act_plane(x, carry):
        rows = at_plane(x, PLANE)
        inputs = feat[rows, :].astype(f32)
        rinv = lax.rsqrt(jnp.mean(inputs * inputs, axis=-1, keepdims=True) + NORM_EPSILON)
        normed = inputs * rinv
        pre = normed * gain[...]
        slope = 1.0 / (1.0 + jnp.exp(-pre))
        kept = mask[rows, :].astype(f32)
        act = (pre * slope * kept).astype(bf16)
        normed_s[rows, :] = normed
        slope_s[rows, :] = kept * (slope * (1.0 + pre * (1.0 - slope))) * gain[...]
        rinv_s[rows, :] = jnp.broadcast_to(rinv, normed.shape)
        a_stack[x, 0:PLANE, :] = act
        a_msg[at_plane(x, EDGE_ROWS), :] = jnp.dot(extract[...], act, preferred_element_type=f32).astype(bf16)
        return carry

    lax.fori_loop(0, BS, act_plane, 0, unroll=2)
    start_deal(1, a_msg)
    loads[3].wait()
    for k in range(1, 8):
        deal_arrival(lax.rem(me + k, 8)).wait_recv()

    def pick_for(slot):
        ym, yp, zn, ymz, ypz, bz = neighbours(slot)
        picked = []
        for p in range(GROUP):
            first = p * EDGE_ROWS
            low, high = slice(first, first + 16), slice(first + 32, first + 48)
            rows = jnp.concatenate(
                [deal[ym, high, :], deal[yp, low, :], deal[zn, first : first + EDGE_ROWS, :], deal[ymz, high, :], deal[ypz, low, :]],
                axis=0,
            )
            picked.append(jnp.dot(compact[bz], rows, preferred_element_type=f32).astype(bf16))
        return jnp.concatenate(picked, axis=0)

    for k in (4, 5, 3, 2, 6, 7, 1):
        slot = lax.rem(me + k, 8)
        deliver[slot] = pick_for(slot)
        halo_copy(k).start()
    halo[core, at_plane(chip, deal_rows), :] = pick_for(me)
    my_height = neighbours(me)[5]
    loads[4].wait()

    def own_plane(x, carry):
        moved = jnp.dot(own_spread[...], a_stack[x, 0:PLANE, :], preferred_element_type=f32).astype(bf16)
        for c in range(3):
            own_wide[at_plane(x, ROWS), c * 128 : (c + 1) * 128] = moved[c * ROWS : (c + 1) * ROWS]
        return carry

    lax.fori_loop(0, BS, own_plane, 0, unroll=2)
    turn = 4 * ROWS
    for i in range(3):
        for c in range(3):
            own_turned[c * 128 : (c + 1) * 128, i * turn : (i + 1) * turn] = own_wide[
                i * turn : (i + 1) * turn, c * 128 : (c + 1) * 128
            ].T

    def widen(which, stack, wide):
        wide[0] = jnp.zeros(wide.shape[1:], bf16)
        wide[BS + 1] = jnp.zeros(wide.shape[1:], bf16)

        def plane(x, carry):
            stack[x, PLANE:STACK, :] = halo[which, at_plane(x, EDGE_ROWS), :]
            moved = jnp.dot(spread[my_height], stack[x], preferred_element_type=f32).astype(bf16)
            for c in range(3):
                wide[x + 1, :, c * 128 : (c + 1) * 128] = moved[c * WIDE : (c + 1) * WIDE]
            return carry

        lax.fori_loop(0, BS, plane, 0, unroll=2)

    loads[5].wait()
    end_halo(0)
    widen(0, g_stack, g_wide)

    def window(a, b):
        return g_wide[1 - a : 1 - a + BS, (1 - b) * ZPAD : (1 - b) * ZPAD + ROWS, 128:256].reshape(BS * ROWS, 128)

    for first in range(0, 9, 2):
        group = list(range(first, min(first + 2, 9)))
        side = [window(*COLUMNS[i]) for i in group]
        rhs = jnp.concatenate(side, axis=1) if len(side) > 1 else side[0]
        term = jnp.dot(own_turned[...], rhs, preferred_element_type=f32)
        for j, i in enumerate(group):
            part[3 * i * 128 : (3 * i + 3) * 128, :] = term[:, j * 128 : (j + 1) * 128]

    def share_of(index):
        return pl.ds(pl.multiple_of(index * share_rows, 16), share_rows)

    def twin_copy(q):
        return remote(part.at[share_of(2 * q + 1 - core)], from_twin.at[q], twin_send.at[q], twin_recv.at[q], region=twin)

    for q in range(chips):
        twin_copy(q).start()

    def z_copy(k):
        target = lax.rem(chip + k, chips)
        return remote(pair16.at[target], from_z.at[k - 1], z_send.at[k - 1], z_recv.at[k - 1], region=2 * target + core)

    for k in (2, 1, 3):
        q = lax.rem(chip + k, chips)
        twin_copy(q).wait_recv()
        pair16[q] = (part[share_of(2 * q + core), :] + from_twin[q]).astype(bf16)
        z_copy(k).start()
    twin_copy(chip).wait_recv()
    pair_own[...] = part[share_of(me), :] + from_twin[chip]

    count = 3

    def convolve_planes(wide, taps, x0, transposed):
        total = None
        for a in range(3):
            lhs = jnp.concatenate(
                [wide[pl.ds(x0 + a, count), b * ZPAD : b * ZPAD + ROWS, :].reshape(count * ROWS, 384) for b in range(3)],
                axis=1,
            )
            if transposed:
                rhs = jnp.concatenate([taps[26 - 9 * a - j] for j in range(9)], axis=1)
                term = lax.dot_general(lhs, rhs, (((1,), (1,)), ((), ())), preferred_element_type=f32)
            else:
                term = jnp.dot(lhs, taps[9 * a : 9 * a + 9].reshape(9 * 128, 128), preferred_element_type=f32)
            total = term if total is None else total + term
        planes = []
        for i in range(count):
            piece = total[i * ROWS : (i + 1) * ROWS]
            high = piece.astype(bf16)
            rest = (piece - high.astype(f32)).astype(bf16)
            planes.append(jnp.dot(squeeze[...], jnp.concatenate([high, rest], axis=0), preferred_element_type=f32))
        return planes

    def backward_planes(step, carry):
        x0 = step * count
        for i, back in enumerate(convolve_planes(g_wide, weight, x0, True)):
            rows = at_plane(x0 + i, PLANE)
            normed = normed_s[rows, :]
            dnorm = back * slope_s[rows, :]
            level = jnp.mean(dnorm * normed, axis=-1, keepdims=True)
            grad_in[rows, :] = (cot[rows, :].astype(f32) + rinv_s[rows, :] * (dnorm - normed * level)).astype(bf16)
        return carry

    loads[6].wait()
    loads[7].wait()
    lax.fori_loop(0, BS // count, backward_planes, 0)

    end_halo(1)
    widen(1, a_stack, a_wide)

    def z_wait(k):
        z_copy(k).wait_recv()

    for k in (1, 3, 2):
        z_wait(k)
    share = pair_own[...] + from_z[0].astype(f32) + from_z[1].astype(f32) + from_z[2].astype(f32)
    squares[me] = jnp.sum((share * share).reshape(share_rows // 8, 8, 128), axis=0)
    shares[scene] = share.astype(bf16)

    def sq_copy(k):
        return remote(squares.at[me], squares.at[me], sq_send.at[k - 1], sq_recv.at[k - 1], region=lax.rem(me + k, 8))

    def sq_arrival(k):
        slot = lax.rem(me + 8 - k, 8)
        return remote(squares.at[slot], squares.at[slot], sq_send.at[k - 1], sq_recv.at[k - 1], region=slot)

    def scene_copy(buf, send, recv, k):
        return remote(buf.at[scene], buf.at[scene], send.at[k - 1], recv.at[k - 1], scene=lax.rem(scene + k, 4))

    def scene_arrival(buf, send, recv, k):
        slot = lax.rem(scene + 4 - k, 4)
        return remote(buf.at[slot], buf.at[slot], send.at[k - 1], recv.at[k - 1], scene=slot)

    for k in range(1, 8):
        sq_copy(k).start()
    for k in range(1, 4):
        scene_copy(shares, sh_send, sh_recv, k).start()

    def forward_planes(step, carry):
        x0 = step * count
        for i, ahead in enumerate(convolve_planes(a_wide, weight, x0, False)):
            rows = at_plane(x0 + i, PLANE)
            out[rows, :] = (feat[rows, :].astype(f32) + ahead * mask[rows, :].astype(f32)).astype(bf16)
        return carry

    lax.fori_loop(0, 1, forward_planes, 0)
    for k in range(1, 8):
        sq_arrival(k).wait_recv()
    total = jnp.sum(jnp.sum(squares[...], axis=0), keepdims=True)
    limit = math.sqrt(TAPS * 128 * 128)
    factors[scene] = jnp.broadcast_to(jnp.minimum(1.0, limit * lax.rsqrt(total)), (8, 128))
    for k in range(1, 4):
        scene_copy(factors, fa_send, fa_recv, k).start()
    lax.fori_loop(1, BS // count, forward_planes, 0)
    for k in range(1, 4):
        scene_arrival(shares, sh_send, sh_recv, k).wait_recv()
        scene_arrival(factors, fa_send, fa_recv, k).wait_recv()
    result = jnp.zeros((share_rows, 128), f32)
    for s in range(4):
        result = result + factors[s, 0:1, :] * shares[s].astype(f32)
    update[...] = result * 0.25

    for which, msg in ((0, g_msg), (1, a_msg)):
        for k in range(1, 4):
            deal_copy(which, msg, k).wait_send()
    for which, msg in ((0, g_msg), (1, a_msg)):

        @pl.when(core != which)
        def _(which=which, msg=msg):
            deal_copy(which, msg, 0).wait_send()

    for k in range(1, 8):
        halo_copy(k).wait_send()
    for q in range(chips):
        twin_copy(q).wait_send()
    for k in range(1, 4):
        z_copy(k).wait_send()
        scene_copy(shares, sh_send, sh_recv, k).wait_send()
        scene_copy(factors, fa_send, fa_recv, k).wait_send()
    for k in range(1, 8):
        sq_copy(k).wait_send()


def fused_body(features, voxel_mask, cotangent, norm_gain, conv_weight, block_owner):
    f32, bf16 = jnp.float32, jnp.bfloat16
    width = features.shape[-1]
    slots = lax.axis_size("region")
    spread = spread_table()
    own = spread[0, :, 1 : 1 + BS, :, :PLANE].reshape(3 * ROWS, PLANE)
    squeeze = np.zeros((BS, BS, BS, ZPAD), np.float32)
    for y in range(BS):
        for z in range(BS):
            squeeze[y, z, y, z + 1] = 1
    squeeze = squeeze.reshape(PLANE, ROWS)
    squeeze = np.concatenate([squeeze, squeeze], axis=1)
    spread = spread.reshape(GZ, 3 * WIDE, STACK)
    voxels = BS * BS * BS
    mask = jnp.broadcast_to(voxel_mask[0, 0].astype(bf16)[:, None], (voxels, width))
    vmem = pl.BlockSpec(memory_space=pltpu.VMEM)
    share_rows = TAPS * width // slots
    sem = pltpu.SemaphoreType.DMA
    tables = [jnp.asarray(table, bf16) for table in (extract_table(), compact_table(), own, spread, squeeze)]
    hbm = [features[0, 0], cotangent[0, 0], conv_weight, *tables]
    out, grad_in, update = pl.pallas_call(
        fused_kernel,
        out_shape=(
            jax.ShapeDtypeStruct((voxels, width), bf16),
            jax.ShapeDtypeStruct((voxels, width), bf16),
            jax.ShapeDtypeStruct((share_rows, width), f32),
        ),
        in_specs=[pl.BlockSpec(memory_space=pltpu.HBM)] * 8 + [vmem, vmem, pl.BlockSpec(memory_space=pltpu.SMEM)],
        out_specs=(vmem, vmem, vmem),
        scratch_shapes=[
            *[pltpu.VMEM(table.shape, bf16) for table in hbm],
            pltpu.VMEM((BS * EDGE_ROWS, width), bf16),
            pltpu.VMEM((BS * EDGE_ROWS, width), bf16),
            pltpu.VMEM((slots + 1, GROUP * EDGE_ROWS, width), bf16),
            pltpu.VMEM((slots, GROUP * EDGE_ROWS, width), bf16),
            pltpu.VMEM((2, BS * EDGE_ROWS, width), bf16),
            pltpu.VMEM((BS, STACK, width), bf16),
            pltpu.VMEM((BS, STACK, width), bf16),
            pltpu.VMEM((BS + 2, WIDE, 3 * width), bf16),
            pltpu.VMEM((BS + 2, WIDE, 3 * width), bf16),
            pltpu.VMEM((BS * ROWS, 3 * width), bf16),
            pltpu.VMEM((3 * width, BS * ROWS), bf16),
            pltpu.VMEM((voxels, width), f32),
            pltpu.VMEM((voxels, width), f32),
            pltpu.VMEM((voxels, width), f32),
            pltpu.VMEM((TAPS * width, width), f32),
            pltpu.VMEM((slots // 2, share_rows, width), f32),
            pltpu.VMEM((slots // 2, share_rows, width), bf16),
            pltpu.VMEM((share_rows, width), f32),
            pltpu.VMEM((slots // 2 - 1, share_rows, width), bf16),
            pltpu.VMEM((slots, 8, width), f32),
            pltpu.VMEM((4, share_rows, width), bf16),
            pltpu.VMEM((4, 8, width), f32),
            sem((8,)),
            sem((2, 4)), sem((slots,)),
            sem((7,)), sem((2, slots // 2)),
            sem((slots // 2,)), sem((slots // 2,)),
            sem((3,)), sem((3,)),
            sem((7,)), sem((7,)),
            sem((3,)), sem((3,)),
            sem((3,)), sem((3,)),
        ],
        compiler_params=pltpu.CompilerParams(
            collective_id=0, has_side_effects=True, vmem_limit_bytes=60 * 1024 * 1024
        ),
        cost_estimate=pl.CostEstimate(flops=5_000_000_000, bytes_accessed=4_000_000, transcendentals=300_000),
    )(
        *hbm, mask, norm_gain[None, :], block_owner,
    )
    return (out.reshape(features.shape), grad_in.reshape(cotangent.shape), update)


def solution(mesh):
    in_specs = (
        P("scene", "region", None, None),
        P("scene", "region", None),
        P("scene", "region", None, None),
        P(),
        P(),
        P("scene", None),
    )
    out_specs = (
        P("scene", "region", None, None),
        P("scene", "region", None, None),
        P("region", None),
    )
    chosen = fused_body if mesh.shape["region"] == GY * GZ else body
    return jax.shard_map(chosen, mesh=mesh, in_specs=in_specs, out_specs=out_specs, check_vma=False)
```
